32 devices in a mesh: section: 4 (over y, x), space: 8 (over z, core).
Axes of the slice: x: 2, y: 2, z: 4, core: 2. Of those that a mesh axis runs over, the one named last changes fastest.
Arguments:
- encoder_inputs: bfloat16 [4, 1, 128, 32, 2, 64], P('section', None, None, 'space'), may hold values from -6 to 6
- upper_inputs: bfloat16 [4, 1, 128, 32, 2, 64], P('section', None, None, 'space'), may hold values from -6 to 6
- output_cotangent: bfloat16 [1, 128, 32, 2, 64], P(None, None, 'space'), may hold values from -6 to 6
- weights: bfloat16 [4, 4, 3, 128, 1152], P('section'), may hold values from -0.15625 to 0.15625
- biases: float32 [4, 4, 128], P('section'), may hold values from -3 to 3
Outputs:
- encoder_grad: bfloat16 [4, 1, 128, 32, 2, 64], P('section', None, None, 'space')
- upper_grad: bfloat16 [4, 1, 128, 32, 2, 64], P('section', None, None, 'space')
- weight_grad: float32 [4, 4, 3, 128, 1152], P('section')
- bias_grad: float32 [4, 4, 128], P('section')
The draws below stay inside these ranges and needn't reach their ends.
All inputs are finite; a program needn't handle non-finite values.
Results may differ from the reference program's by a relative error of at most 0.018.
Values may be sent and summed in bfloat16 or wider, within the bound.
A program may use at most 64 MiB of HBM per device.

```python
import jax
import jax.numpy as jnp
from jax import lax

C = 128
YC = 2
ZC = 64
MICRO = 1
CONVS = 4
SECTIONS = 4
X = 32


def level_of(rng, extent, pieces, least, largest):
    factor_of, own = 1.0, jax.random.fold_in(rng, 6)
    for position, shards_of in pieces:
        draws = jnp.exp(jax.random.uniform(jax.random.fold_in(own, position), (shards_of,), jnp.float32, least / len(pieces), largest / len(pieces)))
        factor_of = factor_of * jnp.repeat(draws, extent[position] // shards_of).reshape([-1 if axis == position else 1 for axis in range(len(extent))])
    return factor_of


def normal_values(key, dims, deviation, limit, pieces=(), held_as=jnp.bfloat16):
    drawn = jax.random.normal(key, dims, jnp.float32) * deviation
    if len(pieces) > 0:
        drawn = level_of(key, dims, pieces, -0.22, 0.18) * drawn
    return jnp.clip(drawn, min=-limit, max=limit).astype(held_as)


def setup_inputs(seed: int = 0) -> dict:
    key_of = jax.random.split(jax.random.key(seed), 6)
    encoder_inputs = normal_values(key_of[0], (SECTIONS, MICRO, C, X, YC, ZC), 1.0, 6.0, ((0, 4), (3, 8)))
    upper_inputs = normal_values(key_of[1], (SECTIONS, MICRO, C, X, YC, ZC), 1.0, 6.0, ((0, 4), (3, 8)))
    output_cotangent = normal_values(key_of[2], (MICRO, C, X, YC, ZC), 1.0, 6.0, ((2, 8),))
    weights = normal_values(key_of[3], (SECTIONS, CONVS, 3, C, 9 * C), (27 * C // 2) ** -0.5, 0.15625, ((0, 4),))
    biases = normal_values(key_of[4], (SECTIONS, CONVS, C), 0.5, 3.0, ((0, 4),), jnp.float32)
    return dict(encoder_inputs=encoder_inputs, upper_inputs=upper_inputs, output_cotangent=output_cotangent, weights=weights, biases=biases)


def rounded(value):
    return lax.optimization_barrier(value.astype(jnp.bfloat16))

def to_kernel(weight):
    width = weight.shape[1]
    return weight.astype(jnp.float32).reshape(3, width, 3, 3, width).transpose(1, 4, 0, 2, 3)

def from_kernel(kernel):
    width = kernel.shape[0]
    return kernel.transpose(2, 0, 3, 4, 1).reshape(3, width, 9 * width)

def convolve(field, kernel):
    return lax.conv_general_dilated(field[None], kernel, (1, 1, 1), [(1, 1), (1, 1), (1, 1)], dimension_numbers=('NCDHW', 'OIDHW', 'NCDHW'), precision=lax.Precision.HIGHEST)[0]

def silu_slope(pre):
    logistic = jax.nn.sigmoid(pre)
    return logistic * (1.0 + pre * (1.0 - logistic))

def block_forward(inputs, first_kernel, second_kernel, first_bias, second_bias):
    first_pre = convolve(inputs.astype(jnp.float32), first_kernel) + first_bias[:, None, None, None]
    first_act = rounded(jax.nn.silu(first_pre))
    second_pre = convolve(first_act.astype(jnp.float32), second_kernel) + second_bias[:, None, None, None]
    return (first_pre, first_act, second_pre)

def block_backward(inputs, first_pre, first_act, second_pre, first_kernel, second_kernel, cotangent):
    second_grad = rounded(cotangent.astype(jnp.float32) * silu_slope(second_pre))
    outputs, pullback = jax.vjp(convolve, first_act.astype(jnp.float32), second_kernel)
    hidden_grad, second_kernel_grad = pullback(second_grad.astype(jnp.float32))
    first_grad = rounded(hidden_grad * silu_slope(first_pre))
    outputs, pullback = jax.vjp(convolve, inputs.astype(jnp.float32), first_kernel)
    input_grad, first_kernel_grad = pullback(first_grad.astype(jnp.float32))
    weight_terms = jnp.stack([from_kernel(first_kernel_grad), from_kernel(second_kernel_grad)])
    bias_terms = jnp.stack([lax.optimization_barrier(jnp.sum(first_grad.astype(jnp.float32), axis=(1, 2, 3))), lax.optimization_barrier(jnp.sum(second_grad.astype(jnp.float32), axis=(1, 2, 3)))])
    return (rounded(input_grad), weight_terms, bias_terms)

def reference(encoder_inputs, upper_inputs, output_cotangent, weights, biases):
    kernels = [[to_kernel(weights[section, layer]) for layer in range(CONVS)] for section in range(SECTIONS)]
    weight_grad = jnp.zeros(weights.shape, jnp.float32)
    bias_grad = jnp.zeros(biases.shape, jnp.float32)
    encoder_list = [[None] * MICRO for section in range(SECTIONS)]
    upper_list = [[None] * MICRO for section in range(SECTIONS)]
    for micro in range(MICRO):
        saved_encoder = []
        saved_decoder = []
        for section in range(SECTIONS):
            inputs = encoder_inputs[section, micro]
            encoded = block_forward(inputs, kernels[section][0], kernels[section][1], biases[section, 0], biases[section, 1])
            encoder_out = rounded(jax.nn.silu(encoded[2]))
            decoder_input = rounded(encoder_out.astype(jnp.float32) + upper_inputs[section, micro].astype(jnp.float32))
            decoded = block_forward(decoder_input, kernels[section][2], kernels[section][3], biases[section, 2], biases[section, 3])
            saved_encoder.append((inputs, encoded[0], encoded[1], encoded[2]))
            saved_decoder.append((decoder_input, decoded[0], decoded[1], decoded[2]))
        cotangent = output_cotangent[micro]
        for section in range(SECTIONS):
            saved = saved_decoder[section]
            input_grad, weight_terms, bias_terms = block_backward(saved[0], saved[1], saved[2], saved[3], kernels[section][2], kernels[section][3], cotangent)
            upper_list[section][micro] = input_grad
            weight_grad = weight_grad.at[section, 2:4].add(weight_terms)
            bias_grad = bias_grad.at[section, 2:4].add(bias_terms)
            cotangent = input_grad
        above = jnp.zeros(output_cotangent.shape[1:], jnp.bfloat16)
        for section in range(SECTIONS - 1, -1, -1):
            cotangent = rounded(upper_list[section][micro].astype(jnp.float32) + above.astype(jnp.float32))
            saved = saved_encoder[section]
            input_grad, weight_terms, bias_terms = block_backward(saved[0], saved[1], saved[2], saved[3], kernels[section][0], kernels[section][1], cotangent)
            encoder_list[section][micro] = input_grad
            weight_grad = weight_grad.at[section, 0:2].add(weight_terms)
            bias_grad = bias_grad.at[section, 0:2].add(bias_terms)
            above = input_grad
    encoder_grad = jnp.stack([jnp.stack(encoder_list[section]) for section in range(SECTIONS)])
    upper_grad = jnp.stack([jnp.stack(upper_list[section]) for section in range(SECTIONS)])
    return (encoder_grad, upper_grad, weight_grad, bias_grad)
```

```python
import functools

import jax
import jax.numpy as jnp
from jax import lax
from jax.experimental import pallas as pl
from jax.experimental.pallas import tpu as pltpu
from jax.sharding import PartitionSpec as P

F32 = jnp.float32
BF16 = jnp.bfloat16


def silu_slope(pre, logistic):
    return logistic * (1.0 + pre * (1.0 - logistic))


def kernel(
    dims,
    x_ref, up_ref, cot_ref, w_ref, bias_ref,
    eg_ref, ug_ref, wg_ref, bg_ref,
    wf, wa, xw, dw, gd, ge, uw, patx, path, patt, s1, s2, sg, fg,
    part, ra, csum, rb, fin,
    send_sem, recv_sem, a_send, a_recv, b_send, b_recv, c_send, c_recv, d_send, d_recv,
):
    S, n, R, Z, Y, C = dims
    F = Y * C
    nz = n // 2
    chunk = csum.shape[1] // nz
    bias_row = 27 * C
    sec = lax.axis_index("section")
    p = lax.axis_index("space")
    core = lax.rem(p, 2)
    chip = lax.div(p, 2)
    partner = p + 1 - 2 * core

    def rows(first, count):
        return pl.ds(first * Z, count * Z)

    def dev(s, q):
        return {"section": s, "space": q}

    def copy(src, dst, ssem, rsem, where):
        return pltpu.make_async_remote_copy(
            src_ref=src, dst_ref=dst, send_sem=ssem, recv_sem=rsem,
            device_id=where, device_id_type=pl.DeviceIdType.MESH,
        )

    has_left, has_right = p > 0, p < n - 1

    for buf in (xw, dw):
        buf[rows(0, R), :] = jnp.zeros((R * Z, F), BF16)
        buf[rows(2 * R, R), :] = jnp.zeros((R * Z, F), BF16)
    for buf in (gd, ge, uw):
        buf[...] = jnp.zeros(buf.shape, BF16)

    barrier = pltpu.get_barrier_semaphore()
    for q in range(n):
        @pl.when(q != p)
        def _():
            pl.semaphore_signal(barrier, inc=1, device_id=dev(sec, q),
                                device_id_type=pl.DeviceIdType.MESH)
    for ds in (-1, 1):
        for dp in (-1, 0, 1):
            ok = (sec + ds >= 0) & (sec + ds < S) & (p + dp >= 0) & (p + dp < n)

            @pl.when(ok)
            def _():
                pl.semaphore_signal(barrier, inc=1, device_id=dev(sec + ds, p + dp),
                                    device_id_type=pl.DeviceIdType.MESH)
    sides = jnp.where(sec > 0, 1, 0) + jnp.where(sec < S - 1, 1, 0)
    wide = 1 + jnp.where(has_left, 1, 0) + jnp.where(has_right, 1, 0)
    pl.semaphore_wait(barrier, n - 1 + sides * wide)

    def spread(srcs, dsts, sids, rids, target, also=True, mid=None):
        left = (also & has_left, lambda: copy(
            srcs[0], dsts[1], send_sem.at[sids[0]], recv_sem.at[rids[1]], dev(target, p - 1)))
        right = (also & has_right, lambda: copy(
            srcs[1], dsts[0], send_sem.at[sids[1]], recv_sem.at[rids[0]], dev(target, p + 1)))
        out = [left, right]
        if mid is not None:
            out.append((also, lambda: copy(
                mid[0], mid[1], send_sem.at[sids[2]], recv_sem.at[rids[2]], dev(target, p))))
        return out

    pending = []

    def start(copies):
        for ok, make in copies:
            @pl.when(ok)
            def _():
                make().start()
        pending.extend(copies)

    def arrive(dst, rid, ok):
        @pl.when(ok)
        def _():
            copy(dst, dst, send_sem.at[rid], recv_sem.at[rid], dev(sec, partner)).wait_recv()

    start(spread((x_ref, x_ref), (xw.at[rows(0, R)], xw.at[rows(2 * R, R)]), (0, 1), (0, 1), sec))
    start(spread((cot_ref.at[rows(0, 2)], cot_ref.at[rows(R - 2, 2)]),
                 (gd.at[rows(0, 2)], gd.at[rows(R + 2, 2)]), (4, 5), (4, 5), sec, also=sec == 0))

    xw[rows(R, R), :] = x_ref[...]

    @pl.when(sec == 0)
    def _():
        gd[rows(2, R), :] = cot_ref[...]

    def build(step, carry):
        l, a = lax.div(step, 3), lax.rem(step, 3)
        for y in range(Y):
            for v in range(Y):
                b = v - y + 1
                for c in range(3):
                    if 0 <= b <= 2:
                        lane = (3 * b + c) * C
                        tap = w_ref[l, a, :, lane:lane + C]
                    else:
                        tap = jnp.zeros((C, C), BF16)
                    wf[l, a, y * C:(y + 1) * C, c * F + v * C:c * F + (v + 1) * C] = tap
                    wa[l, 2 - a, (2 - c) * F + y * C:(2 - c) * F + (y + 1) * C, v * C:(v + 1) * C] = tap
        return carry

    lax.fori_loop(0, w_ref.shape[0] * 3, build, 0)

    def patches(value, pat):
        count = value.shape[0]
        wide_value = value.astype(F32)
        depth = lax.rem(lax.broadcasted_iota(jnp.int32, (count, F), 0), Z)
        low = jnp.where(depth == 0, 0.0, pltpu.roll(wide_value, 1, 0))
        high = jnp.where(depth == Z - 1, 0.0, pltpu.roll(wide_value, count - 1, 0))
        pat[0:count, 0:F] = low.astype(BF16)
        pat[0:count, F:2 * F] = value
        pat[0:count, 2 * F:3 * F] = high.astype(BF16)

    def conv(pat, l, count):
        total = None
        for a in range(3):
            term = lax.dot_general(
                pat[rows(a, count), :], wf[l, a], (((1,), (1,)), ((), ())),
                preferred_element_type=F32)
            total = term if total is None else total + term
        return total

    def conv_back(pat, l, count):
        total = None
        for a in range(3):
            term = jnp.dot(pat[rows(a, count), :], wa[l, a], preferred_element_type=F32)
            total = term if total is None else total + term
        return total

    def inside(count, margin):
        position = lax.div(lax.broadcasted_iota(jnp.int32, (count * Z, F), 0), Z) + p * R - margin
        return (position >= 0) & (position < n * R)

    def bias_of(l):
        one = bias_ref[l:l + 1, :]
        return jnp.concatenate([one] * Y, axis=1)

    def forward(blk, field):
        patches(field, patx.at[blk])
        first = conv(patx.at[blk], 2 * blk, R + 6) + bias_of(2 * blk)
        logistic = jax.nn.sigmoid(first)
        act = jnp.where(inside(R + 6, 3), first * logistic, 0.0).astype(BF16)
        slope = jnp.where(inside(R + 6, 3), silu_slope(first, logistic), 0.0)
        s1[blk] = slope[2 * Z:(R + 4) * Z, :]
        patches(act, path.at[blk])
        second = conv(path.at[blk], 2 * blk + 1, R + 4) + bias_of(2 * blk + 1)
        logistic = jax.nn.sigmoid(second)
        s2[blk] = silu_slope(second, logistic)
        return (second * logistic)[2 * Z:(R + 2) * Z, :].astype(BF16)

    arrive(xw.at[rows(0, R)], 0, has_left)
    arrive(xw.at[rows(2 * R, R)], 1, has_right)
    enc_out = forward(0, xw[...])
    dw[rows(R, R), :] = (enc_out.astype(F32) + up_ref[...].astype(F32)).astype(BF16)
    start(spread((dw.at[rows(R, R)], dw.at[rows(R, R)]),
                 (dw.at[rows(0, R)], dw.at[rows(2 * R, R)]), (2, 3), (2, 3), sec))
    arrive(dw.at[rows(0, R)], 2, has_left)
    arrive(dw.at[rows(2 * R, R)], 3, has_right)
    forward(1, dw[...])

    def backward(blk, cotangent, out_ref):
        second = (cotangent * s2[blk]).astype(BF16)
        sg[blk] = second
        patches(second, patt)
        hidden = conv_back(patt, 2 * blk + 1, R + 2)
        first = (hidden * s1[blk]).astype(BF16)
        fg[blk] = first
        patches(first, patt)
        out_ref[...] = conv_back(patt, 2 * blk, R).astype(BF16)

    def weight_part(blk, layer, grads, pat, offset):
        summed = jnp.sum(grads.astype(F32), axis=0, keepdims=True)
        bias = sum(summed[:, y * C:(y + 1) * C] for y in range(Y))
        extra = csum.shape[1] - bias_row
        part[blk, layer, bias_row:bias_row + extra, :] = jnp.broadcast_to(bias, (extra, C)).astype(BF16)
        turned = grads.astype(F32).T.astype(BF16)
        for a in range(3):
            grid = jnp.dot(turned, pat[rows(offset + a, R), :], preferred_element_type=F32)
            for b in range(3):
                for c in range(3):
                    acc = None
                    for y in range(Y):
                        v = y + b - 1
                        if 0 <= v < Y:
                            term = grid[y * C:(y + 1) * C, c * F + v * C:c * F + (v + 1) * C]
                            acc = term if acc is None else acc + term
                    row = (a * 9 + 3 * b + c) * C
                    part[blk, layer, row:row + C, :] = acc.astype(BF16)

    def stretch(t):
        return pl.ds(pl.multiple_of(t * chunk, 16), chunk)

    def other(j):
        return lax.rem(chip + j, nz)

    def copy_a(blk):
        return copy(part.at[blk, 1 - core], ra.at[blk], a_send.at[blk], a_recv.at[blk],
                    dev(sec, partner))

    def copy_b(blk, t):
        return copy(csum.at[blk, stretch(t)], rb.at[blk, chip], b_send.at[blk, t],
                    b_recv.at[blk, chip], dev(sec, 2 * t + core))

    def copy_c(blk, t):
        here = fin.at[blk, core, stretch(chip)]
        return copy(here, here, c_send.at[blk, t], c_recv.at[blk, chip], dev(sec, 2 * t + core))

    def copy_d(blk, t):
        here = fin.at[blk, core, stretch(t)]
        return copy(here, here, d_send.at[blk, t], d_recv.at[blk, t], dev(sec, partner))

    def reduce_begin(blk):
        weight_part(blk, 1, sg[blk, rows(2, R), :], path.at[blk], 2)
        weight_part(blk, 0, fg[blk, rows(1, R), :], patx.at[blk], R - 1)
        copy_a(blk).start()

    def reduce_pair(blk):
        copy_a(blk).wait_recv()
        csum[blk] = (part[blk, core].astype(F32) + ra[blk].astype(F32)).astype(BF16)
        for j in range(1, nz):
            copy_b(blk, other(j)).start()
        rb[blk, chip] = csum[blk, stretch(chip), :]

    def reduce_chips(blk):
        for j in range(1, nz):
            t = other(j)
            copy(csum.at[blk, stretch(t)], rb.at[blk, t], b_send.at[blk, t],
                 b_recv.at[blk, t], dev(sec, partner)).wait_recv()
        total = rb[blk, 0].astype(F32)
        for t in range(1, nz):
            total = total + rb[blk, t].astype(F32)
        fin[blk, core, stretch(chip), :] = total.astype(BF16)
        for j in range(1, nz):
            copy_c(blk, other(j)).start()
        copy_d(blk, chip).start()

    def gather(blk):
        for j in range(1, nz):
            t = other(j)
            there = fin.at[blk, core, stretch(t)]
            copy(there, there, c_send.at[blk, t], c_recv.at[blk, t], dev(sec, partner)).wait_recv()
            copy_d(blk, t).start()

    def finish(blk):
        for t in range(nz):
            there = fin.at[blk, 1 - core, stretch(t)]
            copy(there, there, d_send.at[blk, t], d_recv.at[blk, t], dev(sec, partner)).wait_recv()
        for layer in range(2):
            for a in range(3):
                for k in range(9):
                    row = (a * 9 + k) * C
                    wg_ref[2 * blk + layer, a, :, k * C:(k + 1) * C] = (
                        fin[blk, layer, row:row + C, :].astype(F32))
            bg_ref[2 * blk + layer:2 * blk + layer + 1, :] = (
                fin[blk, layer, bias_row:bias_row + 16, :].astype(F32)[0:1, :])

    def drain(blk):
        copy_a(blk).wait_send()
        copy_d(blk, chip).wait_send()
        for j in range(1, nz):
            copy_b(blk, other(j)).wait_send()
            copy_c(blk, other(j)).wait_send()
            copy_d(blk, other(j)).wait_send()

    later = sec > 0
    arrive(gd.at[rows(0, 2)], 4, has_left)
    arrive(gd.at[rows(R + 2, 2)], 5, has_right)
    arrive(gd.at[rows(2, R)], 6, later)
    backward(1, gd[...].astype(F32), ug_ref)
    start(spread((ug_ref.at[rows(0, 2)], ug_ref.at[rows(R - 2, 2)]),
                 (gd.at[rows(0, 2)], gd.at[rows(R + 2, 2)]), (6, 7, 8), (4, 5, 6), sec + 1,
                 also=sec < S - 1, mid=(ug_ref, gd.at[rows(2, R)])))
    start(spread((ug_ref.at[rows(0, 2)], ug_ref.at[rows(R - 2, 2)]),
                 (uw.at[rows(0, 2)], uw.at[rows(R + 2, 2)]), (9, 10), (7, 8), sec))
    uw[rows(2, R), :] = ug_ref[...]

    @pl.when(sec < S - 1)
    def _():
        reduce_begin(1)
        reduce_pair(1)

    @pl.when(sec < S - 2)
    def _():
        reduce_chips(1)

    above = sec < S - 1
    arrive(uw.at[rows(0, 2)], 7, has_left)
    arrive(uw.at[rows(R + 2, 2)], 8, has_right)
    arrive(ge.at[rows(0, 2)], 9, above & has_left)
    arrive(ge.at[rows(R + 2, 2)], 10, above & has_right)
    arrive(ge.at[rows(2, R)], 11, above)
    combined = (uw[...].astype(F32) + ge[...].astype(F32)).astype(BF16)
    backward(0, combined.astype(F32), eg_ref)
    start(spread((eg_ref.at[rows(0, 2)], eg_ref.at[rows(R - 2, 2)]),
                 (ge.at[rows(0, 2)], ge.at[rows(R + 2, 2)]), (11, 12, 13), (9, 10, 11), sec - 1,
                 also=sec > 0, mid=(eg_ref, ge.at[rows(2, R)])))

    @pl.when(sec == S - 1)
    def _():
        reduce_begin(1)
        reduce_pair(1)

    reduce_begin(0)
    reduce_pair(0)

    @pl.when(sec >= S - 2)
    def _():
        reduce_chips(1)

    gather(1)
    finish(1)
    reduce_chips(0)
    gather(0)
    finish(0)

    for ok, make in pending:
        @pl.when(ok)
        def _():
            make().wait_send()
    drain(1)
    drain(0)


def on_device(dims, encoder_inputs, upper_inputs, output_cotangent, weights, biases):
    S, n, R, Z, Y, C = dims
    F = Y * C
    nz = n // 2
    unit = 16 * nz
    height = -(-(27 * C + 16) // unit) * unit

    def cells(field):
        return field.transpose(1, 3, 2, 0).reshape(R * Z, F)

    def fields(value):
        return value.reshape(R, Z, Y, C).transpose(3, 0, 2, 1)

    block = jax.ShapeDtypeStruct((R * Z, F), BF16)
    dma = pltpu.SemaphoreType.DMA
    eg, ug, wg, bg = pl.pallas_call(
        functools.partial(kernel, dims),
        out_shape=(
            block, block,
            jax.ShapeDtypeStruct(weights.shape[1:], F32),
            jax.ShapeDtypeStruct(biases.shape[1:], F32),
        ),
        in_specs=[pl.BlockSpec(memory_space=pltpu.VMEM)] * 5,
        out_specs=tuple([pl.BlockSpec(memory_space=pltpu.VMEM)] * 4),
        scratch_shapes=[
            pltpu.VMEM((4, 3, F, 3 * F), BF16),
            pltpu.VMEM((4, 3, 3 * F, F), BF16),
            pltpu.VMEM((3 * R * Z, F), BF16),
            pltpu.VMEM((3 * R * Z, F), BF16),
            pltpu.VMEM(((R + 4) * Z, F), BF16),
            pltpu.VMEM(((R + 4) * Z, F), BF16),
            pltpu.VMEM(((R + 4) * Z, F), BF16),
            pltpu.VMEM((2, (R + 8) * Z, 3 * F), BF16),
            pltpu.VMEM((2, (R + 6) * Z, 3 * F), BF16),
            pltpu.VMEM(((R + 4) * Z, 3 * F), BF16),
            pltpu.VMEM((2, (R + 2) * Z, F), F32),
            pltpu.VMEM((2, (R + 4) * Z, F), F32),
            pltpu.VMEM((2, (R + 4) * Z, F), BF16),
            pltpu.VMEM((2, (R + 2) * Z, F), BF16),
            pltpu.VMEM((2, 2, height, C), BF16),
            pltpu.VMEM((2, height, C), BF16),
            pltpu.VMEM((2, height, C), BF16),
            pltpu.VMEM((2, nz, height // nz, C), BF16),
            pltpu.VMEM((2, 2, height, C), BF16),
            dma((14,)), dma((12,)),
            dma((2,)), dma((2,)),
            dma((2, nz)), dma((2, nz)),
            dma((2, nz)), dma((2, nz)),
            dma((2, nz)), dma((2, nz)),
        ],
        compiler_params=pltpu.CompilerParams(
            collective_id=0, has_side_effects=True, vmem_limit_bytes=58 * 1024 * 1024
        ),
    )(
        cells(encoder_inputs[0, 0]), cells(upper_inputs[0, 0]), cells(output_cotangent[0]),
        weights[0], biases[0],
    )
    return (fields(eg)[None, None], fields(ug)[None, None], wg[None], bg[None])


def solution(mesh):
    def run(encoder_inputs, upper_inputs, output_cotangent, weights, biases):
        channels, total, lateral, depth = encoder_inputs.shape[2:]
        n = mesh.shape["space"]
        dims = (mesh.shape["section"], n, total // n, depth, lateral, channels)
        return jax.shard_map(
            functools.partial(on_device, dims),
            mesh=mesh,
            in_specs=(
                P("section", None, None, "space", None, None),
                P("section", None, None, "space", None, None),
                P(None, None, "space", None, None),
                P("section", None, None, None, None),
                P("section", None, None),
            ),
            out_specs=(
                P("section", None, None, "space", None, None),
                P("section", None, None, "space", None, None),
                P("section", None, None, None, None),
                P("section", None, None),
            ),
            check_vma=False,
        )(encoder_inputs, upper_inputs, output_cotangent, weights, biases)

    return run
```

```python
import functools

import jax
import jax.numpy as jnp
from jax import lax
from jax.experimental import pallas as pl
from jax.experimental.pallas import tpu as pltpu
from jax.sharding import PartitionSpec as P

F32 = jnp.float32
BF16 = jnp.bfloat16


def silu_slope(pre, logistic):
    return logistic * (1.0 + pre * (1.0 - logistic))


def kernel(
    dims,
    x_ref, up_ref, cot_ref, w_ref, bias_ref,
    eg_ref, ug_ref, fin,
    wf, wa, xw, dw, gd, ge, uw, patx, path, patt, s1, s2, sg, fg,
    part, ra, csum, rb,
    send_sem, recv_sem, a_send, a_recv, b_send, b_recv, c_send, c_recv, d_send, d_recv,
):
    S, n, R, Z, Y, C = dims
    F = Y * C
    nz = n // 2
    half = csum.shape[1] // 2
    pieces = b_send.shape[2]
    chunk = half // pieces
    bias_row = 27 * C
    sec = lax.axis_index("section")
    p = lax.axis_index("space")
    core = lax.rem(p, 2)
    chip = lax.div(p, 2)
    partner = p + 1 - 2 * core

    def rows(first, count):
        return pl.ds(first * Z, count * Z)

    def dev(s, q):
        return {"section": s, "space": q}

    def copy(src, dst, ssem, rsem, where):
        return pltpu.make_async_remote_copy(
            src_ref=src, dst_ref=dst, send_sem=ssem, recv_sem=rsem,
            device_id=where, device_id_type=pl.DeviceIdType.MESH,
        )

    has_left, has_right = p > 0, p < n - 1

    for buf in (xw, dw):
        buf[rows(0, R), :] = jnp.zeros((R * Z, F), BF16)
        buf[rows(2 * R, R), :] = jnp.zeros((R * Z, F), BF16)
    for buf in (gd, ge, uw):
        buf[...] = jnp.zeros(buf.shape, BF16)

    barrier = pltpu.get_barrier_semaphore()
    for q in range(n):
        @pl.when(q != p)
        def _():
            pl.semaphore_signal(barrier, inc=1, device_id=dev(sec, q),
                                device_id_type=pl.DeviceIdType.MESH)
    for ds in (-1, 1):
        for dp in (-1, 0, 1):
            ok = (sec + ds >= 0) & (sec + ds < S) & (p + dp >= 0) & (p + dp < n)

            @pl.when(ok)
            def _():
                pl.semaphore_signal(barrier, inc=1, device_id=dev(sec + ds, p + dp),
                                    device_id_type=pl.DeviceIdType.MESH)
    sides = jnp.where(sec > 0, 1, 0) + jnp.where(sec < S - 1, 1, 0)
    wide = 1 + jnp.where(has_left, 1, 0) + jnp.where(has_right, 1, 0)
    pl.semaphore_wait(barrier, n - 1 + sides * wide)

    def spread(srcs, dsts, sids, rids, target, also=True, mid=None):
        left = (also & has_left, lambda: copy(
            srcs[0], dsts[1], send_sem.at[sids[0]], recv_sem.at[rids[1]], dev(target, p - 1)))
        right = (also & has_right, lambda: copy(
            srcs[1], dsts[0], send_sem.at[sids[1]], recv_sem.at[rids[0]], dev(target, p + 1)))
        out = [left, right]
        if mid is not None:
            out.append((also, lambda: copy(
                mid[0], mid[1], send_sem.at[sids[2]], recv_sem.at[rids[2]], dev(target, p))))
        return out

    pending = []

    def start(copies):
        for ok, make in copies:
            @pl.when(ok)
            def _():
                make().start()
        pending.extend(copies)

    def arrive(dst, rid, ok):
        @pl.when(ok)
        def _():
            copy(dst, dst, send_sem.at[rid], recv_sem.at[rid], dev(sec, partner)).wait_recv()

    start(spread((x_ref, x_ref), (xw.at[rows(0, R)], xw.at[rows(2 * R, R)]), (0, 1), (0, 1), sec))
    start(spread((cot_ref.at[rows(0, 2)], cot_ref.at[rows(R - 2, 2)]),
                 (gd.at[rows(0, 2)], gd.at[rows(R + 2, 2)]), (4, 5), (4, 5), sec, also=sec == 0))

    xw[rows(R, R), :] = x_ref[...]

    @pl.when(sec == 0)
    def _():
        gd[rows(2, R), :] = cot_ref[...]

    def build(step, carry):
        l, a = lax.div(step, 3), lax.rem(step, 3)
        for y in range(Y):
            for v in range(Y):
                b = v - y + 1
                for c in range(3):
                    if 0 <= b <= 2:
                        lane = (3 * b + c) * C
                        tap = w_ref[l, a, :, lane:lane + C]
                    else:
                        tap = jnp.zeros((C, C), BF16)
                    wf[l, a, y * C:(y + 1) * C, c * F + v * C:c * F + (v + 1) * C] = tap
                    wa[l, 2 - a, (2 - c) * F + y * C:(2 - c) * F + (y + 1) * C, v * C:(v + 1) * C] = tap
        return carry

    lax.fori_loop(0, w_ref.shape[0] * 3, build, 0)

    def patches(value, pat):
        count = value.shape[0]
        wide_value = value.astype(F32)
        depth = lax.rem(lax.broadcasted_iota(jnp.int32, (count, F), 0), Z)
        low = jnp.where(depth == 0, 0.0, pltpu.roll(wide_value, 1, 0))
        high = jnp.where(depth == Z - 1, 0.0, pltpu.roll(wide_value, count - 1, 0))
        pat[0:count, 0:F] = low.astype(BF16)
        pat[0:count, F:2 * F] = value
        pat[0:count, 2 * F:3 * F] = high.astype(BF16)

    def conv(pat, l, count):
        total = None
        for a in range(3):
            term = lax.dot_general(
                pat[rows(a, count), :], wf[l, a], (((1,), (1,)), ((), ())),
                preferred_element_type=F32)
            total = term if total is None else total + term
        return total

    def conv_back(pat, l, count):
        total = None
        for a in range(3):
            term = jnp.dot(pat[rows(a, count), :], wa[l, a], preferred_element_type=F32)
            total = term if total is None else total + term
        return total

    def inside(count, margin):
        position = lax.div(lax.broadcasted_iota(jnp.int32, (count * Z, F), 0), Z) + p * R - margin
        return (position >= 0) & (position < n * R)

    def bias_of(l):
        one = bias_ref[l:l + 1, :]
        return jnp.concatenate([one] * Y, axis=1)

    def forward(blk, field):
        patches(field, patx.at[blk])
        first = conv(patx.at[blk], 2 * blk, R + 6) + bias_of(2 * blk)
        logistic = jax.nn.sigmoid(first)
        act = jnp.where(inside(R + 6, 3), first * logistic, 0.0).astype(BF16)
        slope = jnp.where(inside(R + 6, 3), silu_slope(first, logistic), 0.0)
        s1[blk] = slope[2 * Z:(R + 4) * Z, :]
        patches(act, path.at[blk])
        second = conv(path.at[blk], 2 * blk + 1, R + 4) + bias_of(2 * blk + 1)
        logistic = jax.nn.sigmoid(second)
        s2[blk] = silu_slope(second, logistic)
        return (second * logistic)[2 * Z:(R + 2) * Z, :].astype(BF16)

    arrive(xw.at[rows(0, R)], 0, has_left)
    arrive(xw.at[rows(2 * R, R)], 1, has_right)
    enc_out = forward(0, xw[...])
    dw[rows(R, R), :] = (enc_out.astype(F32) + up_ref[...].astype(F32)).astype(BF16)
    start(spread((dw.at[rows(R, R)], dw.at[rows(R, R)]),
                 (dw.at[rows(0, R)], dw.at[rows(2 * R, R)]), (2, 3), (2, 3), sec))
    arrive(dw.at[rows(0, R)], 2, has_left)
    arrive(dw.at[rows(2 * R, R)], 3, has_right)
    forward(1, dw[...])

    def backward(blk, cotangent, out_ref):
        second = (cotangent * s2[blk]).astype(BF16)
        sg[blk] = second
        patches(second, patt)
        hidden = conv_back(patt, 2 * blk + 1, R + 2)
        first = (hidden * s1[blk]).astype(BF16)
        fg[blk] = first
        patches(first, patt)
        out_ref[...] = conv_back(patt, 2 * blk, R).astype(BF16)

    def weight_part(blk, layer, grads, pat, offset):
        summed = jnp.sum(grads.astype(F32), axis=0, keepdims=True)
        bias = sum(summed[:, y * C:(y + 1) * C] for y in range(Y))
        extra = csum.shape[1] - bias_row
        part[blk, layer, bias_row:bias_row + extra, :] = jnp.broadcast_to(bias, (extra, C)).astype(BF16)
        turned = grads.astype(F32).T.astype(BF16)
        for a in range(3):
            grid = jnp.dot(turned, pat[rows(offset + a, R), :], preferred_element_type=F32)
            for b in range(3):
                for c in range(3):
                    acc = None
                    for y in range(Y):
                        v = y + b - 1
                        if 0 <= v < Y:
                            term = grid[y * C:(y + 1) * C, c * F + v * C:c * F + (v + 1) * C]
                            acc = term if acc is None else acc + term
                    row = (a * 9 + 3 * b + c) * C
                    part[blk, layer, row:row + C, :] = acc.astype(BF16)

    def stretch(side, i):
        return pl.ds(pl.multiple_of(side * half + i * chunk, 16), chunk)

    ends = (chip == 0, chip == nz - 1)

    def onward(side):
        return dev(sec, p + (4 * side - 2))

    def copy_a(blk):
        return copy(part.at[blk, 1 - core], ra.at[blk], a_send.at[blk], a_recv.at[blk],
                    dev(sec, partner))

    def copy_b(blk, side, i):
        return copy(csum.at[blk, stretch(side, i)], rb.at[blk, stretch(side, i)],
                    b_send.at[blk, side, i], b_recv.at[blk, side, i], onward(side))

    def copy_c(blk, side, i):
        here = fin.at[blk, core, stretch(side, i)]
        return copy(here, here, c_send.at[blk, side, i], c_recv.at[blk, side, i], onward(1 - side))

    def copy_d(blk, side, i, layer):
        here = fin.at[blk, layer, stretch(side, i)]
        return copy(here, here, d_send.at[blk, side, i], d_recv.at[blk, side, i], dev(sec, partner))

    def reduce_begin(blk):
        weight_part(blk, 1, sg[blk, rows(2, R), :], path.at[blk], 2)
        weight_part(blk, 0, fg[blk, rows(1, R), :], patx.at[blk], R - 1)
        copy_a(blk).start()

    def reduce_pair(blk):
        copy_a(blk).wait_recv()
        csum[blk] = (part[blk, core].astype(F32) + ra[blk].astype(F32)).astype(BF16)
        each(lambda i: begin_line(blk, i))

    def begin_line(blk, i):
        for side in range(2):
            @pl.when(ends[1 - side])
            def _():
                copy_b(blk, side, i).start()

    def line_step(blk, t):
        for side in range(2):
            hops = chip if side == 1 else nz - 1 - chip
            i = t - hops

            @pl.when((i >= 0) & (i < pieces) & ~ends[1 - side])
            def _():
                copy_b(blk, side, i).wait_recv()
                here = stretch(side, i)
                total = (csum[blk, here, :].astype(F32) + rb[blk, here, :].astype(F32)).astype(BF16)

                @pl.when(~ends[side])
                def _():
                    csum[blk, here, :] = total
                    copy_b(blk, side, i).start()

                @pl.when(ends[side])
                def _():
                    fin[blk, core, here, :] = total
                    copy_c(blk, side, i).start()
                    copy_d(blk, side, i, core).start()
        for side in range(2):
            hops = chip if side == 1 else nz - 1 - chip
            i = t - 2 * (nz - 1) + hops

            @pl.when((i >= 0) & (i < pieces) & ~ends[side])
            def _():
                copy_c(blk, side, i).wait_recv()

                @pl.when(~ends[1 - side])
                def _():
                    copy_c(blk, side, i).start()
                copy_d(blk, side, i, core).start()

    span = pieces + 2 * (nz - 1)

    def drain_step(blk, i):
        for side in range(2):
            copy_d(blk, side, i, 1 - core).wait_recv()
            copy_d(blk, side, i, core).wait_send()

            @pl.when(~ends[side])
            def _():
                copy_b(blk, side, i).wait_send()

            @pl.when(~ends[1 - side])
            def _():
                copy_c(blk, side, i).wait_send()

    def each(step, count=None):
        def body(i, carry):
            step(i)
            return carry
        lax.fori_loop(0, pieces if count is None else count, body, 0)

    later = sec > 0
    arrive(gd.at[rows(0, 2)], 4, has_left)
    arrive(gd.at[rows(R + 2, 2)], 5, has_right)
    arrive(gd.at[rows(2, R)], 6, later)
    backward(1, gd[...].astype(F32), ug_ref)
    start(spread((ug_ref.at[rows(0, 2)], ug_ref.at[rows(R - 2, 2)]),
                 (gd.at[rows(0, 2)], gd.at[rows(R + 2, 2)]), (6, 7, 8), (4, 5, 6), sec + 1,
                 also=sec < S - 1, mid=(ug_ref, gd.at[rows(2, R)])))
    start(spread((ug_ref.at[rows(0, 2)], ug_ref.at[rows(R - 2, 2)]),
                 (uw.at[rows(0, 2)], uw.at[rows(R + 2, 2)]), (9, 10), (7, 8), sec))
    uw[rows(2, R), :] = ug_ref[...]

    @pl.when(sec < S - 1)
    def _():
        reduce_begin(1)
        reduce_pair(1)

    @pl.when(sec < S - 2)
    def _():
        each(lambda t: line_step(1, t), span)

    above = sec < S - 1
    arrive(uw.at[rows(0, 2)], 7, has_left)
    arrive(uw.at[rows(R + 2, 2)], 8, has_right)
    arrive(ge.at[rows(0, 2)], 9, above & has_left)
    arrive(ge.at[rows(R + 2, 2)], 10, above & has_right)
    arrive(ge.at[rows(2, R)], 11, above)
    combined = (uw[...].astype(F32) + ge[...].astype(F32)).astype(BF16)
    backward(0, combined.astype(F32), eg_ref)
    start(spread((eg_ref.at[rows(0, 2)], eg_ref.at[rows(R - 2, 2)]),
                 (ge.at[rows(0, 2)], ge.at[rows(R + 2, 2)]), (11, 12, 13), (9, 10, 11), sec - 1,
                 also=sec > 0, mid=(eg_ref, ge.at[rows(2, R)])))

    @pl.when(sec == S - 1)
    def _():
        reduce_begin(1)
        reduce_pair(1)

    reduce_begin(0)
    reduce_pair(0)

    @pl.when(sec >= S - 2)
    def _():
        def both(t):
            line_step(1, t)
            line_step(0, t - pieces)
        each(both, span + pieces)

    @pl.when(sec < S - 2)
    def _():
        each(lambda t: line_step(0, t), span)

    for ok, make in pending:
        @pl.when(ok)
        def _():
            make().wait_send()
    for blk in range(2):
        copy_a(blk).wait_send()
        each(lambda i: drain_step(blk, i))


def spread_out(fin_ref, out_ref):
    C = fin_ref.shape[3]
    taps = out_ref.shape[3] // C
    for a in range(3):
        for k in range(taps):
            row = (a * taps + k) * C
            out_ref[0, a, :, k * C:(k + 1) * C] = fin_ref[0, 0, row:row + C, :].astype(F32)


def on_device(dims, encoder_inputs, upper_inputs, output_cotangent, weights, biases):
    S, n, R, Z, Y, C = dims
    F = Y * C
    pieces = 7
    unit = 32 * pieces
    height = -(-(27 * C + 16) // unit) * unit

    def cells(field):
        return field.transpose(1, 3, 2, 0).reshape(R * Z, F)

    def fields(value):
        return value.reshape(R, Z, Y, C).transpose(3, 0, 2, 1)

    block = jax.ShapeDtypeStruct((R * Z, F), BF16)
    dma = pltpu.SemaphoreType.DMA
    eg, ug, total = pl.pallas_call(
        functools.partial(kernel, dims),
        out_shape=(
            block, block,
            jax.ShapeDtypeStruct((2, 2, height, C), BF16),
        ),
        in_specs=[pl.BlockSpec(memory_space=pltpu.VMEM)] * 5,
        out_specs=tuple([pl.BlockSpec(memory_space=pltpu.VMEM)] * 3),
        scratch_shapes=[
            pltpu.VMEM((4, 3, F, 3 * F), BF16),
            pltpu.VMEM((4, 3, 3 * F, F), BF16),
            pltpu.VMEM((3 * R * Z, F), BF16),
            pltpu.VMEM((3 * R * Z, F), BF16),
            pltpu.VMEM(((R + 4) * Z, F), BF16),
            pltpu.VMEM(((R + 4) * Z, F), BF16),
            pltpu.VMEM(((R + 4) * Z, F), BF16),
            pltpu.VMEM((2, (R + 8) * Z, 3 * F), BF16),
            pltpu.VMEM((2, (R + 6) * Z, 3 * F), BF16),
            pltpu.VMEM(((R + 4) * Z, 3 * F), BF16),
            pltpu.VMEM((2, (R + 2) * Z, F), F32),
            pltpu.VMEM((2, (R + 4) * Z, F), F32),
            pltpu.VMEM((2, (R + 4) * Z, F), BF16),
            pltpu.VMEM((2, (R + 2) * Z, F), BF16),
            pltpu.VMEM((2, 2, height, C), BF16),
            pltpu.VMEM((2, height, C), BF16),
            pltpu.VMEM((2, height, C), BF16),
            pltpu.VMEM((2, height, C), BF16),
            dma((14,)), dma((12,)),
            dma((2,)), dma((2,)),
            dma((2, 2, pieces)), dma((2, 2, pieces)),
            dma((2, 2, pieces)), dma((2, 2, pieces)),
            dma((2, 2, pieces)), dma((2, 2, pieces)),
        ],
        compiler_params=pltpu.CompilerParams(
            collective_id=0, has_side_effects=True, vmem_limit_bytes=58 * 1024 * 1024
        ),
    )(
        cells(encoder_inputs[0, 0]), cells(upper_inputs[0, 0]), cells(output_cotangent[0]),
        weights[0], biases[0],
    )
    wg = pl.pallas_call(
        spread_out,
        grid=(2, 2),
        out_shape=jax.ShapeDtypeStruct(weights.shape[1:], F32),
        in_specs=[pl.BlockSpec((1, 1, 27 * C, C), lambda i, j: (i, j, 0, 0))],
        out_specs=pl.BlockSpec((1,) + weights.shape[2:], lambda i, j: (2 * i + j, 0, 0, 0)),
        compiler_params=pltpu.CompilerParams(vmem_limit_bytes=16 * 1024 * 1024),
    )(total)
    bg = total[:, :, 27 * C, :].reshape(4, C).astype(F32)
    return (fields(eg)[None, None], fields(ug)[None, None], wg[None], bg[None])


def solution(mesh):
    def run(encoder_inputs, upper_inputs, output_cotangent, weights, biases):
        channels, total, lateral, depth = encoder_inputs.shape[2:]
        n = mesh.shape["space"]
        dims = (mesh.shape["section"], n, total // n, depth, lateral, channels)
        return jax.shard_map(
            functools.partial(on_device, dims),
            mesh=mesh,
            in_specs=(
                P("section", None, None, "space", None, None),
                P("section", None, None, "space", None, None),
                P(None, None, "space", None, None),
                P("section", None, None, None, None),
                P("section", None, None),
            ),
            out_specs=(
                P("section", None, None, "space", None, None),
                P("section", None, None, "space", None, None),
                P("section", None, None, None, None),
                P("section", None, None),
            ),
            check_vma=False,
        )(encoder_inputs, upper_inputs, output_cotangent, weights, biases)

    return run
```
